32 devices in a mesh: groups: 2 (over y), fsdp: 4 (over z), dp: 2 (over x), seq: 2 (over core).
Axes of the slice: x: 2, y: 2, z: 4, core: 2. Of those that a mesh axis runs over, the one named last changes fastest.
Arguments:
- tokens: bfloat16 [4096, 8192], P(('groups', 'fsdp', 'dp', 'seq')), parts along dimension 0, may hold values from -6 to 6
- cotangent: bfloat16 [4096, 1024], P(('groups', 'fsdp', 'dp', 'seq')), parts along dimension 0, may hold values from -6 to 6
- frozen_key_weight: bfloat16 [8192, 1024], P('fsdp'), may hold values from -0.0625 to 0.0625
- adapter_down_weight: bfloat16 [4, 16, 8192], P('fsdp', None, ('dp', 'seq')), may hold values from -0.0625 to 0.0625
- adapter_up_weight: bfloat16 [4, 16, 1024], P('fsdp', None, ('dp', 'seq')), may hold values from -0.1875 to 0.1875
- tenant_block_tiles: int32 [8], P('groups'), parts along dimension 0, may hold values from 1 to 12, 16 in all
- tenant_owner_slot: int32 [4], replicated, may hold values from 0 to 3, each once
Outputs:
- input_row_gradient: bfloat16 [4096, 8192], P(('groups', 'fsdp', 'dp', 'seq')), parts along dimension 0
- grad_down: float32 [8, 16, 8192], P(('groups', 'fsdp'), None, ('dp', 'seq')), parts along dimension 0
- grad_up: float32 [8, 16, 1024], P(('groups', 'fsdp'), None, ('dp', 'seq')), parts along dimension 0
The draws below stay inside these ranges and needn't reach their ends.
There are 2 independent parts, one for each index of `groups`. The reference program is written for one: setup_inputs(seed, part) draws one part's arguments, and reference() takes and returns one part's arrays. A program takes and returns all parts, laid end to end along the dimension named above; an argument that names none is the same for every part. Nothing has to cross between parts.
Inputs may be any that keep to these rules, and one draw needn't show every extreme that they name: `tenant_block_tiles`: blocks of 128-row tiles laid end to end in tenant order, summing to 16 tiles; the largest block has exactly 12 tiles. `tenant_owner_slot`: A permutation; slot s lies on fsdp index s.
All inputs are finite; a program needn't handle non-finite values.
Results may differ from the reference program's by a relative error of at most 0.005.
Values may be sent and summed in bfloat16 or wider, within the bound.
A program may use at most 64 MiB of HBM per device.

```python
import math
import jax
import jax.numpy as jnp
import numpy as np
from jax import lax

MODEL_WIDTH = 8192
KEY_WIDTH = 1024
ADAPTER_RANK = 16
TILE = 128
TENANT_SLOTS = 4
TILES = 16
TOKENS = 2048
MOST = 12


def block_scale(rng, dims, cuts, least, high):
    gain = 1.0
    for axis_at, parts in cuts:
        draws = jax.random.uniform(jax.random.fold_in(jax.random.fold_in(rng, 6), axis_at), (parts,), jnp.float32, least / len(cuts), high / len(cuts))
        gain = gain * jnp.repeat(jnp.exp(draws), dims[axis_at] // parts).reshape((-1,) + (1,) * (len(dims) - 1 - axis_at))
    return gain


def split_up(number_of, total, reach, slope):
    weights = [(1 << 20) // math.isqrt(rank ** slope) + 1 for rank in range(2, number_of + 1)]
    spare, given = total - reach - (number_of - 1), [1] * (number_of - 1)
    while spare > 0:
        candidates = [i for i in range(number_of - 1) if given[i] < reach]
        pool, budget = sum([weights[i] for i in candidates]), spare
        for i in candidates:
            extra = min(reach - given[i], max(1, budget * weights[i] // pool), spare)
            given[i] = given[i] + extra
            spare = spare - extra
    return np.array([reach] + given)


def ragged_sizes(own_key, number_of, total, limit, lean):
    if number_of == 2:
        one = jax.random.randint(own_key, (), max(1, total - limit), min(limit, total - 1) + 1)
        return jnp.stack([one, total - one])
    sizes = jnp.asarray(split_up(number_of, total, limit, lean), jnp.int32)
    pairs = (number_of - 1) // 2
    donor, receiver = sizes[1:1 + 2 * pairs:2], sizes[2:2 + 2 * pairs:2]
    margin = jnp.minimum(donor - 1, limit - receiver)
    passed = jax.random.randint(jax.random.fold_in(own_key, 1), (pairs,), 0, 1 << 20) % (margin + 1)
    sizes = sizes.at[1:1 + 2 * pairs:2].set(donor - passed).at[2:2 + 2 * pairs:2].set(receiver + passed)
    return sizes[jax.random.permutation(jax.random.fold_in(own_key, 2), number_of)]


def centred(stream_key, dims, width, most, shards=(), kind=jnp.bfloat16):
    values = width * jax.random.normal(stream_key, dims, jnp.float32)
    if shards:
        values = values * block_scale(stream_key, dims, shards, -0.22, 0.18)
    return jnp.clip(values, -most, most).astype(kind)


def setup_inputs(seed: int = 0, part: int = 0) -> dict:
    key_of = jax.random.split(jax.random.key(seed), 8)
    part_keys = jax.random.split(jax.random.fold_in(key_of[7], part), 8)
    return {
        "tokens": centred(part_keys[0], (TOKENS, MODEL_WIDTH), 1.0, 6.0, ((0, 16),)),
        "cotangent": centred(part_keys[1], (TOKENS, KEY_WIDTH), 1.0, 6.0, ((0, 16),)),
        "frozen_key_weight": centred(key_of[2], (MODEL_WIDTH, KEY_WIDTH), MODEL_WIDTH ** -0.5, 0.0625, ((0, 4),)),
        "adapter_down_weight": centred(key_of[3], (TENANT_SLOTS, ADAPTER_RANK, MODEL_WIDTH), MODEL_WIDTH ** -0.5, 0.0625, ((0, 4), (2, 4))),
        "adapter_up_weight": centred(key_of[4], (TENANT_SLOTS, ADAPTER_RANK, KEY_WIDTH), KEY_WIDTH ** -0.5, 0.1875, ((0, 4), (2, 4))),
        "tenant_block_tiles": ragged_sizes(part_keys[5], TENANT_SLOTS, TILES, MOST, 2).astype(jnp.int32),
        "tenant_owner_slot": jax.random.permutation(key_of[6], TENANT_SLOTS).astype(jnp.int32),
    }


def tile_slots(tenant_block_tiles, tenant_owner_slot):
    bounds = jnp.cumsum(tenant_block_tiles).astype(jnp.int32)
    positions = jnp.arange(TILES, dtype=jnp.int32)
    tenant = jnp.sum((bounds[None, :] <= positions[:, None]).astype(jnp.int32), axis=1).astype(jnp.int32)
    return tenant_owner_slot[tenant].astype(jnp.int32)


def reference(tokens, cotangent, frozen_key_weight, adapter_down_weight, adapter_up_weight, tenant_block_tiles, tenant_owner_slot):
    slot_ids = tile_slots(tenant_block_tiles, tenant_owner_slot)
    tok_tiles = tokens.reshape(TILES, TILE, MODEL_WIDTH)
    cot_tiles = cotangent.reshape(TILES, TILE, KEY_WIDTH)
    trailing = (((1,), (1,)), ((), ()))
    leading = (((0,), (0,)), ((), ()))

    def one_tile(items):
        rows, grads, adapter_slot = items
        down_projected = adapter_down_weight[adapter_slot]
        upper_limit = adapter_up_weight[adapter_slot]
        frozen_part = lax.dot_general(grads, frozen_key_weight, trailing, preferred_element_type=jnp.float32).astype(jnp.bfloat16)
        lower_limit = lax.dot_general(grads, upper_limit, trailing, preferred_element_type=jnp.float32).astype(jnp.bfloat16)
        inner = lax.dot_general(rows, down_projected, trailing, preferred_element_type=jnp.float32).astype(jnp.bfloat16)
        result = (frozen_part.astype(jnp.float32) + jnp.dot(lower_limit, down_projected, preferred_element_type=jnp.float32)).astype(jnp.bfloat16)
        part_down = lax.dot_general(lower_limit, rows, leading, preferred_element_type=jnp.float32)
        part_up = lax.dot_general(inner, grads, leading, preferred_element_type=jnp.float32)
        return result, part_down, part_up

    results, parts_down, parts_up = lax.map(one_tile, (tok_tiles, cot_tiles, slot_ids))
    sums_down = jax.ops.segment_sum(parts_down, slot_ids, num_segments=TENANT_SLOTS)
    sums_up = jax.ops.segment_sum(parts_up, slot_ids, num_segments=TENANT_SLOTS)
    counts = jnp.zeros((TENANT_SLOTS,), jnp.float32).at[tenant_owner_slot].set(tenant_block_tiles.astype(jnp.float32))
    return results.reshape(TOKENS, MODEL_WIDTH), sums_down / counts[:, None, None], sums_up / counts[:, None, None]
```

```python
import functools

import jax
import jax.numpy as jnp
from jax import lax
from jax.experimental import pallas as pl
from jax.experimental.pallas import tpu as pltpu
from jax.sharding import PartitionSpec as P

MESH = pl.DeviceIdType.MESH
TRAILING = (((1,), (1,)), ((), ()))
LEADING = (((0,), (0,)), ((), ()))


def kernel(
    n,
    dp_size,
    seq_size,
    tiles_ref,
    owner_ref,
    tok_hbm,
    cot_hbm,
    weight_hbm,
    down_hbm,
    up_hbm,
    out_hbm,
    low_out,
    down_out,
    grad_down,
    grad_up,
    weight,
    tok,
    cot_all,
    ad_all,
    res,
    pick,
    mine,
    part_send,
    part_recv,
    sum_send,
    sum_recv,
    local_sem,
    cot_send_sem,
    cot_recv_sem,
    ad_send_sem,
    ad_recv_sem,
    res_send_sem,
    res_recv_sem,
    pick_send_sem,
    pick_recv_sem,
    part_send_sem,
    part_recv_sem,
    sum_send_sem,
    sum_recv_sem,
):
    peers = dp_size * seq_size
    z = lax.axis_index("fsdp")
    p = lax.axis_index("dp") * seq_size + lax.axis_index("seq")
    tenants = owner_ref.shape[0]
    width = weight.shape[0]
    wide = down_hbm.shape[2]
    chunk = min(512, width)

    def along(index):
        return {"fsdp": index}

    def peer(index):
        return {"dp": index // seq_size, "seq": index % seq_size}

    def remote(src, dst, send, recv, device):
        return pltpu.make_async_remote_copy(
            src_ref=src, dst_ref=dst, send_sem=send, recv_sem=recv, device_id=device, device_id_type=MESH
        )

    load_down = pltpu.make_async_copy(down_hbm.at[0], ad_all.at[z, :, pl.ds(0, wide)], local_sem.at[0])
    load_up = pltpu.make_async_copy(
        up_hbm.at[0], ad_all.at[z, :, pl.ds(wide, up_hbm.shape[2])], local_sem.at[1]
    )
    load_cot = pltpu.make_async_copy(cot_hbm, cot_all.at[z], local_sem.at[2])
    load_weight = pltpu.make_async_copy(weight_hbm, weight, local_sem.at[3])
    load_tok = pltpu.make_async_copy(tok_hbm, tok, local_sem.at[4])
    load_down.start()
    load_up.start()
    load_cot.start()
    load_weight.start()
    load_tok.start()

    barrier = pltpu.get_barrier_semaphore()
    for i in range(1, n):
        pl.semaphore_signal(barrier, inc=1, device_id=along(lax.rem(z + i, n)), device_id_type=MESH)
    for j in range(1, peers):
        pl.semaphore_signal(barrier, inc=1, device_id=peer(lax.rem(p + j, peers)), device_id_type=MESH)
    load_down.wait()
    load_up.wait()
    pl.semaphore_wait(barrier, n - 1 + peers - 1)

    def valid(direction, k):
        return (z - k >= 0) if direction == 0 else (z + k <= n - 1)

    def more(direction):
        return (z < n - 1) if direction == 0 else (z > 0)

    def onward(direction):
        return jnp.minimum(z + 1, n - 1) if direction == 0 else jnp.maximum(z - 1, 0)

    def source(direction, k):
        return jnp.maximum(z - k, 0) if direction == 0 else jnp.minimum(z + k, n - 1)

    def ad_hop(direction, k):
        block = z if k == 0 else source(direction, k)
        return remote(
            ad_all.at[block],
            ad_all.at[block],
            ad_send_sem.at[direction, k],
            ad_recv_sem.at[direction, k + 1],
            along(onward(direction)),
        )

    def cot_hop(direction, k):
        block = z if k == 0 else source(direction, k)
        return remote(
            cot_hbm if k == 0 else cot_all.at[block],
            cot_all.at[block],
            cot_send_sem.at[direction, k],
            cot_recv_sem.at[direction, k + 1],
            along(onward(direction)),
        )

    def arrived(direction, k, buffer, send, recv):
        block = source(direction, k)
        remote(
            buffer.at[block], buffer.at[block], send.at[direction, k], recv.at[direction, k], along(onward(direction))
        ).wait_recv()

    def out_columns(index):
        return out_hbm.at[:, pl.ds(pl.multiple_of(index * width, 128), width)]

    def result(direction, k):
        block = source(direction, k)
        return remote(
            res.at[block],
            out_columns(z),
            res_send_sem.at[direction, k],
            res_recv_sem.at[direction, k],
            along(block),
        )

    def product(block):
        def body(i, carry):
            at = pl.ds(pl.multiple_of(i * chunk, chunk), chunk)
            res[block, :, at] = lax.dot_general(
                cot_all[block], weight[at, :], TRAILING, preferred_element_type=jnp.float32
            ).astype(jnp.bfloat16)
            return carry

        lax.fori_loop(0, width // chunk, body, 0)

    for direction in (0, 1):

        @pl.when(more(direction))
        def _():
            ad_hop(direction, 0).start()
            cot_hop(direction, 0).start()

    load_cot.wait()
    load_weight.wait()
    product(z)
    own_out = pltpu.make_async_copy(res.at[z], out_columns(z), local_sem.at[5])
    own_out.start()

    for k in range(1, n):
        for direction in (0, 1):

            @pl.when(valid(direction, k))
            def _():
                arrived(direction, k, ad_all, ad_send_sem, ad_recv_sem)
                if k < n - 1:

                    @pl.when(more(direction))
                    def _():
                        ad_hop(direction, k).start()

                arrived(direction, k, cot_all, cot_send_sem, cot_recv_sem)
                if k < n - 1:

                    @pl.when(more(direction))
                    def _():
                        cot_hop(direction, k).start()

        for direction in (0, 1):

            @pl.when(valid(direction, k))
            def _():
                product(source(direction, k))
                result(direction, k).start()

    def slot_of(j):
        position = z * peers + lax.rem(p + j, peers)
        low, slot = jnp.int32(0), jnp.int32(0)
        for t in range(tenants):
            high = low + tiles_ref[t]
            inside = jnp.logical_and(position >= low, position < high)
            slot = slot + jnp.where(inside, owner_ref[t], 0)
            low = high
        return slot

    slots = [slot_of(j) for j in range(peers)]

    def chosen(j):
        total = None
        for s in range(n):
            term = jnp.where(slots[j] == s, 1.0, 0.0) * ad_all[s].astype(jnp.float32)
            total = term if total is None else total + term
        return total.astype(jnp.bfloat16)

    def pick_copy(j):
        return remote(
            pick.at[j], mine.at[p], pick_send_sem.at[j], pick_recv_sem.at[j], peer(lax.rem(p + j, peers))
        )

    for j in range(1, peers):
        pick[j] = chosen(j)
        pick_copy(j).start()
    mine[p] = chosen(0)
    for j in range(1, peers):
        came = lax.rem(p + peers - j, peers)
        remote(mine.at[came], mine.at[came], pick_send_sem.at[j], pick_recv_sem.at[j], peer(came)).wait_recv()

    load_tok.wait()
    low_t = jnp.zeros(low_out.shape, jnp.float32)
    inner_t = jnp.zeros(low_out.shape, jnp.float32)
    narrow = mine.shape[2] - wide
    for q in range(peers):
        low_t += lax.dot_general(
            mine[q, :, wide:],
            cot_all[z, :, q * narrow : (q + 1) * narrow],
            TRAILING,
            preferred_element_type=jnp.float32,
        )
    for q in range(peers):
        inner_t += lax.dot_general(
            mine[q, :, :wide],
            tok[:, q * wide : (q + 1) * wide],
            TRAILING,
            preferred_element_type=jnp.float32,
        )
        down_out[:, q * wide : (q + 1) * wide] = mine[q, :, :wide]
    low_t = low_t.astype(jnp.bfloat16)
    inner_t = inner_t.astype(jnp.bfloat16)
    low_out[...] = low_t

    def part_copy(j):
        return remote(
            part_send.at[j],
            part_recv.at[j],
            part_send_sem.at[j],
            part_recv_sem.at[j],
            peer(lax.rem(p + j, peers)),
        )

    def part(j, target):
        q = lax.rem(p + j, peers)
        target[j, :, :wide] = jnp.dot(
            low_t,
            tok[:, pl.ds(pl.multiple_of(q * wide, 128), wide)],
            preferred_element_type=jnp.float32,
        )
        target[j, :, wide:] = jnp.dot(
            inner_t,
            cot_all[z, :, pl.ds(pl.multiple_of(q * narrow, 128), narrow)],
            preferred_element_type=jnp.float32,
        )

    for j in range(1, peers):
        part(j, part_send)
        part_copy(j).start()
    part(0, part_recv)
    for j in range(1, peers):
        part_copy(j).wait_recv()

    def slot_sum(s):
        total = None
        for j in range(peers):
            term = jnp.where(slots[(peers - j) % peers] == s, 1.0, 0.0) * part_recv[j]
            total = term if total is None else total + term
        return total

    def sum_copy(i):
        return remote(
            sum_send.at[i], sum_recv.at[i], sum_send_sem.at[i], sum_recv_sem.at[i], along(lax.rem(z + i, n))
        )

    for i in range(1, n):
        sum_send[i] = slot_sum(lax.rem(z + i, n)).astype(jnp.bfloat16)
        sum_copy(i).start()
    total = slot_sum(z)
    for i in range(1, n):
        sum_copy(i).wait_recv()
        total = total + sum_recv[i].astype(jnp.float32)
    grad_down[...] = total[:, :wide]
    grad_up[...] = total[:, wide:]

    for k in range(1, n):
        for direction in (0, 1):
            @pl.when(valid(1 - direction, k))
            def _():
                came = source(1 - direction, k)
                remote(
                    res.at[came],
                    out_columns(came),
                    res_send_sem.at[direction, k],
                    res_recv_sem.at[direction, k],
                    along(came),
                ).wait_recv()

    own_out.wait()
    for direction in (0, 1):
        for k in range(n - 1):

            @pl.when(jnp.logical_and(more(direction), valid(direction, k)))
            def _():
                ad_hop(direction, k).wait_send()
                cot_hop(direction, k).wait_send()

        for k in range(1, n):

            @pl.when(valid(direction, k))
            def _():
                result(direction, k).wait_send()

    for j in range(1, peers):
        pick_copy(j).wait_send()
        part_copy(j).wait_send()
    for i in range(1, n):
        sum_copy(i).wait_send()


def local(
    n,
    dp_size,
    seq_size,
    tokens,
    cotangent,
    frozen_key_weight,
    adapter_down_weight,
    adapter_up_weight,
    tenant_block_tiles,
    tenant_owner_slot,
):
    peers = dp_size * seq_size
    rows, model = tokens.shape
    keys = cotangent.shape[1]
    width = frozen_key_weight.shape[0]
    _, rank, wide = adapter_down_weight.shape
    narrow = adapter_up_weight.shape[2]
    both = wide + narrow
    bf16, f32 = jnp.bfloat16, jnp.float32
    vmem = pl.BlockSpec(memory_space=pltpu.VMEM)
    smem = pl.BlockSpec(memory_space=pltpu.SMEM)
    anywhere = pl.BlockSpec(memory_space=pl.ANY)
    dma = pltpu.SemaphoreType.DMA
    frozen_part, low_t, down, sum_down, sum_up = pl.pallas_call(
        functools.partial(kernel, n, dp_size, seq_size),
        out_shape=(
            jax.ShapeDtypeStruct((rows, model), bf16),
            jax.ShapeDtypeStruct((rank, rows), bf16),
            jax.ShapeDtypeStruct((rank, model), bf16),
            jax.ShapeDtypeStruct((rank, wide), f32),
            jax.ShapeDtypeStruct((rank, narrow), f32),
        ),
        in_specs=[smem, smem, anywhere, anywhere, anywhere, anywhere, anywhere],
        out_specs=(anywhere, vmem, vmem, vmem, vmem),
        scratch_shapes=[
            pltpu.VMEM((width, keys), bf16),
            pltpu.VMEM((rows, model), bf16),
            pltpu.VMEM((n, rows, keys), bf16),
            pltpu.VMEM((n, rank, both), bf16),
            pltpu.VMEM((n, rows, width), bf16),
            pltpu.VMEM((peers, rank, both), bf16),
            pltpu.VMEM((peers, rank, both), bf16),
            pltpu.VMEM((peers, rank, both), f32),
            pltpu.VMEM((peers, rank, both), f32),
            pltpu.VMEM((n, rank, both), bf16),
            pltpu.VMEM((n, rank, both), bf16),
            dma((6,)),
            dma((2, n)),
            dma((2, n + 1)),
            dma((2, n)),
            dma((2, n + 1)),
            dma((2, n)),
            dma((2, n)),
            dma((peers,)),
            dma((peers,)),
            dma((peers,)),
            dma((peers,)),
            dma((n,)),
            dma((n,)),
        ],
        compiler_params=pltpu.CompilerParams(
            collective_id=0, has_side_effects=True, vmem_limit_bytes=56 * 1024 * 1024
        ),
        cost_estimate=pl.CostEstimate(
            flops=2 * n * rows * keys * width, bytes_accessed=16 * 1024 * 1024, transcendentals=0
        ),
    )(
        tenant_block_tiles,
        tenant_owner_slot,
        tokens,
        cotangent,
        frozen_key_weight,
        adapter_down_weight,
        adapter_up_weight,
    )
    adapter_part = lax.dot_general(low_t, down, LEADING, preferred_element_type=f32)
    input_row_gradient = (frozen_part.astype(f32) + adapter_part).astype(bf16)
    mine = tenant_owner_slot == lax.axis_index("fsdp")
    tile_total = jnp.sum(jnp.where(mine, tenant_block_tiles, 0)).astype(f32)
    return (input_row_gradient, (sum_down / tile_total)[None], (sum_up / tile_total)[None])


def solution(mesh):
    placed = (
        P(("groups", "fsdp", "dp", "seq"), None),
        P(("groups", "fsdp", "dp", "seq"), None),
        P("fsdp", None),
        P("fsdp", None, ("dp", "seq")),
        P("fsdp", None, ("dp", "seq")),
        P("groups"),
        P(),
    )
    sizes = (mesh.shape["fsdp"], mesh.shape["dp"], mesh.shape["seq"])
    return jax.shard_map(
        functools.partial(local, *sizes),
        mesh=mesh,
        in_specs=placed,
        out_specs=(
            P(("groups", "fsdp", "dp", "seq"), None),
            P(("groups", "fsdp"), None, ("dp", "seq")),
            P(("groups", "fsdp"), None, ("dp", "seq")),
        ),
        check_vma=False,
    )
```

```python
import functools

import jax
import jax.numpy as jnp
from jax import lax
from jax.experimental import pallas as pl
from jax.experimental.pallas import tpu as pltpu
from jax.sharding import PartitionSpec as P

MESH = pl.DeviceIdType.MESH
TRAILING = (((1,), (1,)), ((), ()))
LEADING = (((0,), (0,)), ((), ()))


def kernel(
    n,
    dp_size,
    seq_size,
    tiles_ref,
    owner_ref,
    tok_hbm,
    cot_hbm,
    weight_hbm,
    down_hbm,
    up_hbm,
    out_hbm,
    low_out,
    down_out,
    grad_down,
    grad_up,
    weight,
    tok,
    cot_all,
    ad_all,
    res,
    pick,
    mine,
    part_send,
    part_recv,
    sum_send,
    sum_recv,
    local_sem,
    cot_send_sem,
    cot_recv_sem,
    ad_send_sem,
    ad_recv_sem,
    res_send_sem,
    res_recv_sem,
    pick_send_sem,
    pick_recv_sem,
    part_send_sem,
    part_recv_sem,
    sum_send_sem,
    sum_recv_sem,
):
    peers = dp_size * seq_size
    z = lax.axis_index("fsdp")
    p = lax.axis_index("dp") * seq_size + lax.axis_index("seq")
    tenants = owner_ref.shape[0]
    width = weight.shape[0]
    wide = down_hbm.shape[2]
    chunk = min(512, width)

    def along(index):
        return {"fsdp": index}

    def peer(index):
        return {"dp": index // seq_size, "seq": index % seq_size}

    def remote(src, dst, send, recv, device):
        return pltpu.make_async_remote_copy(
            src_ref=src, dst_ref=dst, send_sem=send, recv_sem=recv, device_id=device, device_id_type=MESH
        )

    load_down = pltpu.make_async_copy(down_hbm.at[0], ad_all.at[z, :, pl.ds(0, wide)], local_sem.at[0])
    load_up = pltpu.make_async_copy(
        up_hbm.at[0], ad_all.at[z, :, pl.ds(wide, up_hbm.shape[2])], local_sem.at[1]
    )
    load_cot = pltpu.make_async_copy(cot_hbm, cot_all.at[z], local_sem.at[2])
    load_weight = pltpu.make_async_copy(weight_hbm, weight, local_sem.at[3])
    load_tok = pltpu.make_async_copy(tok_hbm, tok, local_sem.at[4])
    load_down.start()
    load_up.start()
    load_cot.start()
    load_weight.start()
    load_tok.start()

    barrier = pltpu.get_barrier_semaphore()
    for i in range(1, n):
        pl.semaphore_signal(barrier, inc=1, device_id=along(lax.rem(z + i, n)), device_id_type=MESH)
    for j in range(1, peers):
        pl.semaphore_signal(barrier, inc=1, device_id=peer(lax.rem(p + j, peers)), device_id_type=MESH)
    load_down.wait()
    load_up.wait()
    pl.semaphore_wait(barrier, n - 1 + peers - 1)

    def valid(direction, k):
        return (z - k >= 0) if direction == 0 else (z + k <= n - 1)

    def more(direction):
        return (z < n - 1) if direction == 0 else (z > 0)

    def onward(direction):
        return jnp.minimum(z + 1, n - 1) if direction == 0 else jnp.maximum(z - 1, 0)

    def source(direction, k):
        return jnp.maximum(z - k, 0) if direction == 0 else jnp.minimum(z + k, n - 1)

    def ad_hop(direction, k):
        block = z if k == 0 else source(direction, k)
        return remote(
            ad_all.at[block],
            ad_all.at[block],
            ad_send_sem.at[direction, k],
            ad_recv_sem.at[direction, k + 1],
            along(onward(direction)),
        )

    def cot_hop(direction, k):
        block = z if k == 0 else source(direction, k)
        return remote(
            cot_hbm if k == 0 else cot_all.at[block],
            cot_all.at[block],
            cot_send_sem.at[direction, k],
            cot_recv_sem.at[direction, k + 1],
            along(onward(direction)),
        )

    def arrived(direction, k, buffer, send, recv):
        block = source(direction, k)
        remote(
            buffer.at[block], buffer.at[block], send.at[direction, k], recv.at[direction, k], along(onward(direction))
        ).wait_recv()

    def out_columns(index):
        return out_hbm.at[:, pl.ds(pl.multiple_of(index * width, 128), width)]

    def result(direction, k):
        block = source(direction, k)
        return remote(
            res.at[block],
            out_columns(z),
            res_send_sem.at[direction, k],
            res_recv_sem.at[direction, k],
            along(block),
        )

    def product(block):
        def body(i, carry):
            at = pl.ds(pl.multiple_of(i * chunk, chunk), chunk)
            res[block, :, at] = lax.dot_general(
                cot_all[block], weight[at, :], TRAILING, preferred_element_type=jnp.float32
            ).astype(jnp.bfloat16)
            return carry

        lax.fori_loop(0, width // chunk, body, 0)

    for direction in (0, 1):

        @pl.when(more(direction))
        def _():
            ad_hop(direction, 0).start()
            cot_hop(direction, 0).start()

    load_cot.wait()
    load_weight.wait()
    product(z)
    own_out = pltpu.make_async_copy(res.at[z], out_columns(z), local_sem.at[5])
    own_out.start()

    for k in range(1, n):
        for direction in (0, 1):

            @pl.when(valid(direction, k))
            def _():
                arrived(direction, k, ad_all, ad_send_sem, ad_recv_sem)
                if k < n - 1:

                    @pl.when(more(direction))
                    def _():
                        ad_hop(direction, k).start()

                arrived(direction, k, cot_all, cot_send_sem, cot_recv_sem)
                if k < n - 1:

                    @pl.when(more(direction))
                    def _():
                        cot_hop(direction, k).start()

        for direction, now in ((1, z < n // 2), (0, z >= 0), (1, z >= n // 2)):

            @pl.when(jnp.logical_and(valid(direction, k), now))
            def _():
                product(source(direction, k))
                result(direction, k).start()

    def slot_of(j):
        position = z * peers + lax.rem(p + j, peers)
        low, slot = jnp.int32(0), jnp.int32(0)
        for t in range(tenants):
            high = low + tiles_ref[t]
            inside = jnp.logical_and(position >= low, position < high)
            slot = slot + jnp.where(inside, owner_ref[t], 0)
            low = high
        return slot

    slots = [slot_of(j) for j in range(peers)]

    def chosen(j):
        total = None
        for s in range(n):
            term = jnp.where(slots[j] == s, 1.0, 0.0) * ad_all[s].astype(jnp.float32)
            total = term if total is None else total + term
        return total.astype(jnp.bfloat16)

    def pick_copy(j):
        return remote(
            pick.at[j], mine.at[p], pick_send_sem.at[j], pick_recv_sem.at[j], peer(lax.rem(p + j, peers))
        )

    for j in range(1, peers):
        pick[j] = chosen(j)
        pick_copy(j).start()
    mine[p] = chosen(0)
    for j in range(1, peers):
        came = lax.rem(p + peers - j, peers)
        remote(mine.at[came], mine.at[came], pick_send_sem.at[j], pick_recv_sem.at[j], peer(came)).wait_recv()

    load_tok.wait()
    low_t = jnp.zeros(low_out.shape, jnp.float32)
    inner_t = jnp.zeros(low_out.shape, jnp.float32)
    narrow = mine.shape[2] - wide
    for q in range(peers):
        low_t += lax.dot_general(
            mine[q, :, wide:],
            cot_all[z, :, q * narrow : (q + 1) * narrow],
            TRAILING,
            preferred_element_type=jnp.float32,
        )
    for q in range(peers):
        inner_t += lax.dot_general(
            mine[q, :, :wide],
            tok[:, q * wide : (q + 1) * wide],
            TRAILING,
            preferred_element_type=jnp.float32,
        )
        down_out[:, q * wide : (q + 1) * wide] = mine[q, :, :wide]
    low_t = low_t.astype(jnp.bfloat16)
    inner_t = inner_t.astype(jnp.bfloat16)
    low_out[...] = low_t

    def part_copy(j):
        return remote(
            part_send.at[j],
            part_recv.at[j],
            part_send_sem.at[j],
            part_recv_sem.at[j],
            peer(lax.rem(p + j, peers)),
        )

    def part(j, target):
        q = lax.rem(p + j, peers)
        target[j, :, :wide] = jnp.dot(
            low_t,
            tok[:, pl.ds(pl.multiple_of(q * wide, 128), wide)],
            preferred_element_type=jnp.float32,
        )
        target[j, :, wide:] = jnp.dot(
            inner_t,
            cot_all[z, :, pl.ds(pl.multiple_of(q * narrow, 128), narrow)],
            preferred_element_type=jnp.float32,
        )

    for j in range(1, peers):
        part(j, part_send)
        part_copy(j).start()
    part(0, part_recv)
    for j in range(1, peers):
        part_copy(j).wait_recv()

    def slot_sum(s):
        total = None
        for j in range(peers):
            term = jnp.where(slots[(peers - j) % peers] == s, 1.0, 0.0) * part_recv[j]
            total = term if total is None else total + term
        return total

    def sum_copy(i):
        return remote(
            sum_send.at[i], sum_recv.at[i], sum_send_sem.at[i], sum_recv_sem.at[i], along(lax.rem(z + i, n))
        )

    for i in range(1, n):
        sum_send[i] = slot_sum(lax.rem(z + i, n)).astype(jnp.bfloat16)
        sum_copy(i).start()
    total = slot_sum(z)
    for i in range(1, n):
        sum_copy(i).wait_recv()
        total = total + sum_recv[i].astype(jnp.float32)
    count = jnp.int32(0)
    for t in range(tenants):
        count = count + jnp.where(owner_ref[t] == z, tiles_ref[t], 0)
    total = total / count.astype(jnp.float32)
    grad_down[0] = total[:, :wide]
    grad_up[0] = total[:, wide:]

    for k in range(1, n):
        for direction in (0, 1):
            @pl.when(valid(1 - direction, k))
            def _():
                came = source(1 - direction, k)
                remote(
                    res.at[came],
                    out_columns(came),
                    res_send_sem.at[direction, k],
                    res_recv_sem.at[direction, k],
                    along(came),
                ).wait_recv()

    own_out.wait()
    for direction in (0, 1):
        for k in range(n - 1):

            @pl.when(jnp.logical_and(more(direction), valid(direction, k)))
            def _():
                ad_hop(direction, k).wait_send()
                cot_hop(direction, k).wait_send()

        for k in range(1, n):

            @pl.when(valid(direction, k))
            def _():
                result(direction, k).wait_send()

    for j in range(1, peers):
        pick_copy(j).wait_send()
        part_copy(j).wait_send()
    for i in range(1, n):
        sum_copy(i).wait_send()


def local(
    n,
    dp_size,
    seq_size,
    tokens,
    cotangent,
    frozen_key_weight,
    adapter_down_weight,
    adapter_up_weight,
    tenant_block_tiles,
    tenant_owner_slot,
):
    peers = dp_size * seq_size
    rows, model = tokens.shape
    keys = cotangent.shape[1]
    width = frozen_key_weight.shape[0]
    _, rank, wide = adapter_down_weight.shape
    narrow = adapter_up_weight.shape[2]
    both = wide + narrow
    bf16, f32 = jnp.bfloat16, jnp.float32
    vmem = pl.BlockSpec(memory_space=pltpu.VMEM)
    smem = pl.BlockSpec(memory_space=pltpu.SMEM)
    anywhere = pl.BlockSpec(memory_space=pl.ANY)
    dma = pltpu.SemaphoreType.DMA
    frozen_part, low_t, down, mean_down, mean_up = pl.pallas_call(
        functools.partial(kernel, n, dp_size, seq_size),
        out_shape=(
            jax.ShapeDtypeStruct((rows, model), bf16),
            jax.ShapeDtypeStruct((rank, rows), bf16),
            jax.ShapeDtypeStruct((rank, model), bf16),
            jax.ShapeDtypeStruct((1, rank, wide), f32),
            jax.ShapeDtypeStruct((1, rank, narrow), f32),
        ),
        in_specs=[smem, smem, anywhere, anywhere, anywhere, anywhere, anywhere],
        out_specs=(anywhere, vmem, vmem, vmem, vmem),
        scratch_shapes=[
            pltpu.VMEM((width, keys), bf16),
            pltpu.VMEM((rows, model), bf16),
            pltpu.VMEM((n, rows, keys), bf16),
            pltpu.VMEM((n, rank, both), bf16),
            pltpu.VMEM((n, rows, width), bf16),
            pltpu.VMEM((peers, rank, both), bf16),
            pltpu.VMEM((peers, rank, both), bf16),
            pltpu.VMEM((peers, rank, both), f32),
            pltpu.VMEM((peers, rank, both), f32),
            pltpu.VMEM((n, rank, both), bf16),
            pltpu.VMEM((n, rank, both), bf16),
            dma((6,)),
            dma((2, n)),
            dma((2, n + 1)),
            dma((2, n)),
            dma((2, n + 1)),
            dma((2, n)),
            dma((2, n)),
            dma((peers,)),
            dma((peers,)),
            dma((peers,)),
            dma((peers,)),
            dma((n,)),
            dma((n,)),
        ],
        compiler_params=pltpu.CompilerParams(
            collective_id=0, has_side_effects=True, vmem_limit_bytes=56 * 1024 * 1024
        ),
        cost_estimate=pl.CostEstimate(
            flops=2 * n * rows * keys * width, bytes_accessed=16 * 1024 * 1024, transcendentals=0
        ),
    )(
        tenant_block_tiles,
        tenant_owner_slot,
        tokens,
        cotangent,
        frozen_key_weight,
        adapter_down_weight,
        adapter_up_weight,
    )
    adapter_part = lax.dot_general(low_t, down, LEADING, preferred_element_type=f32)
    input_row_gradient = (frozen_part.astype(f32) + adapter_part).astype(bf16)
    return (input_row_gradient, mean_down, mean_up)


def solution(mesh):
    placed = (
        P(("groups", "fsdp", "dp", "seq"), None),
        P(("groups", "fsdp", "dp", "seq"), None),
        P("fsdp", None),
        P("fsdp", None, ("dp", "seq")),
        P("fsdp", None, ("dp", "seq")),
        P("groups"),
        P(),
    )
    sizes = (mesh.shape["fsdp"], mesh.shape["dp"], mesh.shape["seq"])
    return jax.shard_map(
        functools.partial(local, *sizes),
        mesh=mesh,
        in_specs=placed,
        out_specs=(
            P(("groups", "fsdp", "dp", "seq"), None),
            P(("groups", "fsdp"), None, ("dp", "seq")),
            P(("groups", "fsdp"), None, ("dp", "seq")),
        ),
        check_vma=False,
    )
```

```python
import functools

import jax
import jax.numpy as jnp
from jax import lax
from jax.experimental import pallas as pl
from jax.experimental.pallas import tpu as pltpu
from jax.sharding import PartitionSpec as P

MESH = pl.DeviceIdType.MESH
TRAILING = (((1,), (1,)), ((), ()))
LEADING = (((0,), (0,)), ((), ()))


def kernel(
    n,
    dp_size,
    seq_size,
    tiles_ref,
    owner_ref,
    tok_hbm,
    cot_hbm,
    weight_hbm,
    down_hbm,
    up_hbm,
    out_hbm,
    low_out,
    down_out,
    grad_down,
    grad_up,
    weight,
    tok,
    cot_all,
    ad_all,
    res,
    pick,
    mine,
    part_send,
    part_recv,
    sum_send,
    sum_recv,
    local_sem,
    cot_send_sem,
    cot_recv_sem,
    ad_send_sem,
    ad_recv_sem,
    res_send_sem,
    res_recv_sem,
    pick_send_sem,
    pick_recv_sem,
    part_send_sem,
    part_recv_sem,
    sum_send_sem,
    sum_recv_sem,
):
    peers = dp_size * seq_size
    z = lax.axis_index("fsdp")
    p = lax.axis_index("dp") * seq_size + lax.axis_index("seq")
    tenants = owner_ref.shape[0]
    width = weight.shape[0]
    wide = down_hbm.shape[2]
    chunk = min(512, width)

    def along(index):
        return {"fsdp": index}

    def peer(index):
        return {"dp": index // seq_size, "seq": index % seq_size}

    def remote(src, dst, send, recv, device):
        return pltpu.make_async_remote_copy(
            src_ref=src, dst_ref=dst, send_sem=send, recv_sem=recv, device_id=device, device_id_type=MESH
        )

    load_down = pltpu.make_async_copy(down_hbm.at[0], ad_all.at[z, :, pl.ds(0, wide)], local_sem.at[0])
    load_up = pltpu.make_async_copy(
        up_hbm.at[0], ad_all.at[z, :, pl.ds(wide, up_hbm.shape[2])], local_sem.at[1]
    )
    load_cot = pltpu.make_async_copy(cot_hbm, cot_all.at[z], local_sem.at[2])
    load_weight = pltpu.make_async_copy(weight_hbm, weight, local_sem.at[3])
    load_tok = pltpu.make_async_copy(tok_hbm, tok, local_sem.at[4])
    load_down.start()
    load_up.start()
    load_cot.start()
    load_weight.start()
    load_tok.start()

    barrier = pltpu.get_barrier_semaphore()
    for i in range(1, n):
        pl.semaphore_signal(barrier, inc=1, device_id=along(lax.rem(z + i, n)), device_id_type=MESH)
    for j in range(1, peers):
        pl.semaphore_signal(barrier, inc=1, device_id=peer(lax.rem(p + j, peers)), device_id_type=MESH)
    load_down.wait()
    load_up.wait()
    pl.semaphore_wait(barrier, n - 1 + peers - 1)

    def valid(direction, k):
        return (z - k >= 0) if direction == 0 else (z + k <= n - 1)

    def more(direction):
        return (z < n - 1) if direction == 0 else (z > 0)

    def onward(direction):
        return jnp.minimum(z + 1, n - 1) if direction == 0 else jnp.maximum(z - 1, 0)

    def source(direction, k):
        return jnp.maximum(z - k, 0) if direction == 0 else jnp.minimum(z + k, n - 1)

    def ad_hop(direction, k):
        block = z if k == 0 else source(direction, k)
        return remote(
            ad_all.at[block],
            ad_all.at[block],
            ad_send_sem.at[direction, k],
            ad_recv_sem.at[direction, k + 1],
            along(onward(direction)),
        )

    def cot_hop(direction, k):
        block = z if k == 0 else source(direction, k)
        return remote(
            cot_hbm if k == 0 else cot_all.at[block],
            cot_all.at[block],
            cot_send_sem.at[direction, k],
            cot_recv_sem.at[direction, k + 1],
            along(onward(direction)),
        )

    def arrived(direction, k, buffer, send, recv):
        block = source(direction, k)
        remote(
            buffer.at[block], buffer.at[block], send.at[direction, k], recv.at[direction, k], along(onward(direction))
        ).wait_recv()

    def out_columns(index):
        return out_hbm.at[:, pl.ds(pl.multiple_of(index * width, 128), width)]

    def result(direction, k):
        block = source(direction, k)
        return remote(
            res.at[block],
            out_columns(z),
            res_send_sem.at[direction, k],
            res_recv_sem.at[direction, k],
            along(block),
        )

    def product(block):
        def body(i, carry):
            at = pl.ds(pl.multiple_of(i * chunk, chunk), chunk)
            res[block, :, at] = lax.dot_general(
                cot_all[block], weight[at, :], TRAILING, preferred_element_type=jnp.float32
            ).astype(jnp.bfloat16)
            return carry

        lax.fori_loop(0, width // chunk, body, 0)

    for direction in (0, 1):

        @pl.when(more(direction))
        def _():
            ad_hop(direction, 0).start()
            cot_hop(direction, 0).start()

    load_cot.wait()
    load_weight.wait()
    product(z)
    own_out = pltpu.make_async_copy(res.at[z], out_columns(z), local_sem.at[5])
    own_out.start()

    for k in range(1, n):
        for direction in (0, 1):

            @pl.when(valid(direction, k))
            def _():
                arrived(direction, k, ad_all, ad_send_sem, ad_recv_sem)
                if k < n - 1:

                    @pl.when(more(direction))
                    def _():
                        ad_hop(direction, k).start()

    def step(k):
        for direction in (0, 1):

            @pl.when(valid(direction, k))
            def _():
                arrived(direction, k, cot_all, cot_send_sem, cot_recv_sem)
                if k < n - 1:

                    @pl.when(more(direction))
                    def _():
                        cot_hop(direction, k).start()

        for direction, now in ((1, z < n // 2), (0, z >= 0), (1, z >= n // 2)):

            @pl.when(jnp.logical_and(valid(direction, k), now))
            def _():
                product(source(direction, k))
                result(direction, k).start()

    def slot_of(j):
        position = z * peers + lax.rem(p + j, peers)
        low, slot = jnp.int32(0), jnp.int32(0)
        for t in range(tenants):
            high = low + tiles_ref[t]
            inside = jnp.logical_and(position >= low, position < high)
            slot = slot + jnp.where(inside, owner_ref[t], 0)
            low = high
        return slot

    slots = [slot_of(j) for j in range(peers)]

    def chosen(j):
        total = None
        for s in range(n):
            term = jnp.where(slots[j] == s, 1.0, 0.0) * ad_all[s].astype(jnp.float32)
            total = term if total is None else total + term
        return total.astype(jnp.bfloat16)

    def pick_copy(j):
        return remote(
            pick.at[j], mine.at[p], pick_send_sem.at[j], pick_recv_sem.at[j], peer(lax.rem(p + j, peers))
        )

    for j in range(1, peers):
        pick[j] = chosen(j)
        pick_copy(j).start()
    mine[p] = chosen(0)
    step(1)
    for j in range(1, peers):
        came = lax.rem(p + peers - j, peers)
        remote(mine.at[came], mine.at[came], pick_send_sem.at[j], pick_recv_sem.at[j], peer(came)).wait_recv()

    load_tok.wait()
    low_t = jnp.zeros(low_out.shape, jnp.float32)
    inner_t = jnp.zeros(low_out.shape, jnp.float32)
    narrow = mine.shape[2] - wide
    for q in range(peers):
        low_t += lax.dot_general(
            mine[q, :, wide:],
            cot_all[z, :, q * narrow : (q + 1) * narrow],
            TRAILING,
            preferred_element_type=jnp.float32,
        )
    for q in range(peers):
        inner_t += lax.dot_general(
            mine[q, :, :wide],
            tok[:, q * wide : (q + 1) * wide],
            TRAILING,
            preferred_element_type=jnp.float32,
        )
        down_out[:, q * wide : (q + 1) * wide] = mine[q, :, :wide]
    low_t = low_t.astype(jnp.bfloat16)
    inner_t = inner_t.astype(jnp.bfloat16)
    low_out[...] = low_t

    def part_copy(j):
        return remote(
            part_send.at[j],
            part_recv.at[j],
            part_send_sem.at[j],
            part_recv_sem.at[j],
            peer(lax.rem(p + j, peers)),
        )

    def part(j, target):
        q = lax.rem(p + j, peers)
        target[j, :, :wide] = jnp.dot(
            low_t,
            tok[:, pl.ds(pl.multiple_of(q * wide, 128), wide)],
            preferred_element_type=jnp.float32,
        )
        target[j, :, wide:] = jnp.dot(
            inner_t,
            cot_all[z, :, pl.ds(pl.multiple_of(q * narrow, 128), narrow)],
            preferred_element_type=jnp.float32,
        )

    for j in range(1, peers):
        part(j, part_send)
        part_copy(j).start()
    part(0, part_recv)
    for k in range(2, n):
        step(k)
    for j in range(1, peers):
        part_copy(j).wait_recv()

    def slot_sum(s):
        total = None
        for j in range(peers):
            term = jnp.where(slots[(peers - j) % peers] == s, 1.0, 0.0) * part_recv[j]
            total = term if total is None else total + term
        return total

    def sum_copy(i):
        return remote(
            sum_send.at[i], sum_recv.at[i], sum_send_sem.at[i], sum_recv_sem.at[i], along(lax.rem(z + i, n))
        )

    for i in range(1, n):
        sum_send[i] = slot_sum(lax.rem(z + i, n)).astype(jnp.bfloat16)
        sum_copy(i).start()
    total = slot_sum(z)
    for i in range(1, n):
        sum_copy(i).wait_recv()
        total = total + sum_recv[i].astype(jnp.float32)
    count = jnp.int32(0)
    for t in range(tenants):
        count = count + jnp.where(owner_ref[t] == z, tiles_ref[t], 0)
    total = total / count.astype(jnp.float32)
    grad_down[0] = total[:, :wide]
    grad_up[0] = total[:, wide:]

    for k in range(1, n):
        for direction in (0, 1):
            @pl.when(valid(1 - direction, k))
            def _():
                came = source(1 - direction, k)
                remote(
                    res.at[came],
                    out_columns(came),
                    res_send_sem.at[direction, k],
                    res_recv_sem.at[direction, k],
                    along(came),
                ).wait_recv()

    own_out.wait()
    for direction in (0, 1):
        for k in range(n - 1):

            @pl.when(jnp.logical_and(more(direction), valid(direction, k)))
            def _():
                ad_hop(direction, k).wait_send()
                cot_hop(direction, k).wait_send()

        for k in range(1, n):

            @pl.when(valid(direction, k))
            def _():
                result(direction, k).wait_send()

    for j in range(1, peers):
        pick_copy(j).wait_send()
        part_copy(j).wait_send()
    for i in range(1, n):
        sum_copy(i).wait_send()


def local(
    n,
    dp_size,
    seq_size,
    tokens,
    cotangent,
    frozen_key_weight,
    adapter_down_weight,
    adapter_up_weight,
    tenant_block_tiles,
    tenant_owner_slot,
):
    peers = dp_size * seq_size
    rows, model = tokens.shape
    keys = cotangent.shape[1]
    width = frozen_key_weight.shape[0]
    _, rank, wide = adapter_down_weight.shape
    narrow = adapter_up_weight.shape[2]
    both = wide + narrow
    bf16, f32 = jnp.bfloat16, jnp.float32
    vmem = pl.BlockSpec(memory_space=pltpu.VMEM)
    smem = pl.BlockSpec(memory_space=pltpu.SMEM)
    anywhere = pl.BlockSpec(memory_space=pl.ANY)
    dma = pltpu.SemaphoreType.DMA
    frozen_part, low_t, down, mean_down, mean_up = pl.pallas_call(
        functools.partial(kernel, n, dp_size, seq_size),
        out_shape=(
            jax.ShapeDtypeStruct((rows, model), bf16),
            jax.ShapeDtypeStruct((rank, rows), bf16),
            jax.ShapeDtypeStruct((rank, model), bf16),
            jax.ShapeDtypeStruct((1, rank, wide), f32),
            jax.ShapeDtypeStruct((1, rank, narrow), f32),
        ),
        in_specs=[smem, smem, anywhere, anywhere, anywhere, anywhere, anywhere],
        out_specs=(anywhere, vmem, vmem, vmem, vmem),
        scratch_shapes=[
            pltpu.VMEM((width, keys), bf16),
            pltpu.VMEM((rows, model), bf16),
            pltpu.VMEM((n, rows, keys), bf16),
            pltpu.VMEM((n, rank, both), bf16),
            pltpu.VMEM((n, rows, width), bf16),
            pltpu.VMEM((peers, rank, both), bf16),
            pltpu.VMEM((peers, rank, both), bf16),
            pltpu.VMEM((peers, rank, both), f32),
            pltpu.VMEM((peers, rank, both), f32),
            pltpu.VMEM((n, rank, both), bf16),
            pltpu.VMEM((n, rank, both), bf16),
            dma((6,)),
            dma((2, n)),
            dma((2, n + 1)),
            dma((2, n)),
            dma((2, n + 1)),
            dma((2, n)),
            dma((2, n)),
            dma((peers,)),
            dma((peers,)),
            dma((peers,)),
            dma((peers,)),
            dma((n,)),
            dma((n,)),
        ],
        compiler_params=pltpu.CompilerParams(
            collective_id=0, has_side_effects=True, vmem_limit_bytes=56 * 1024 * 1024
        ),
        cost_estimate=pl.CostEstimate(
            flops=2 * n * rows * keys * width, bytes_accessed=16 * 1024 * 1024, transcendentals=0
        ),
    )(
        tenant_block_tiles,
        tenant_owner_slot,
        tokens,
        cotangent,
        frozen_key_weight,
        adapter_down_weight,
        adapter_up_weight,
    )
    adapter_part = lax.dot_general(low_t, down, LEADING, preferred_element_type=f32)
    input_row_gradient = (frozen_part.astype(f32) + adapter_part).astype(bf16)
    return (input_row_gradient, mean_down, mean_up)


def solution(mesh):
    placed = (
        P(("groups", "fsdp", "dp", "seq"), None),
        P(("groups", "fsdp", "dp", "seq"), None),
        P("fsdp", None),
        P("fsdp", None, ("dp", "seq")),
        P("fsdp", None, ("dp", "seq")),
        P("groups"),
        P(),
    )
    sizes = (mesh.shape["fsdp"], mesh.shape["dp"], mesh.shape["seq"])
    return jax.shard_map(
        functools.partial(local, *sizes),
        mesh=mesh,
        in_specs=placed,
        out_specs=(
            P(("groups", "fsdp", "dp", "seq"), None),
            P(("groups", "fsdp"), None, ("dp", "seq")),
            P(("groups", "fsdp"), None, ("dp", "seq")),
        ),
        check_vma=False,
    )
```
